32 devices in a mesh: row: 4 (over y, x), col: 4 (over z), depth: 2 (over core).
Axes of the slice: x: 2, y: 2, z: 4, core: 2. Of those that a mesh axis runs over, the one named last changes fastest.
Arguments:
- node_features: bfloat16 [4096, 512], P(('row', 'col'), 'depth'), may hold values from -6 to 6
- weight: bfloat16 [512, 512], P('depth'), may hold values from -0.25 to 0.25
- cotangent: bfloat16 [4096, 512], P(('row', 'col'), 'depth'), may hold values from -6 to 6
- diffusion_time: float32 [1], replicated, may hold values from 0.5 to 2
- tile_count: int32 [4, 4], P('row', 'col'), may hold values from 2 to 24, as said below
- tile_row: int32 [4, 4, 24], P('row', 'col'), may hold values from 0 to 3, as said below
- tile_col: int32 [4, 4, 24], P('row', 'col'), may hold values from 0 to 3, as said below
- tile_vals: bfloat16 [4, 4, 24, 256, 256], P('row', 'col'), may hold values from -0.07782233 to 0.07782233, as said below
Outputs:
- grad_features: bfloat16 [4096, 512], P(('row', 'col'), 'depth')
- grad_weight: float32 [512, 512], P('depth')
The draws below stay inside these ranges and needn't reach their ends.
Inputs may be any that keep to these rules, and one draw needn't show every extreme that they name: Block (r, c) uses its slots 0 to tile_count[r, c] - 1; the largest count, 24, is reached by some block in every draw. `tile_row`: tile rows index the 4 tile rows of the block's node-row range; positions may repeat. `tile_col`: tile columns index the 4 tile columns of the block; positions may repeat. `tile_vals`: edge weights, about half of them zero.
All inputs are finite; a program needn't handle non-finite values.
Results may differ from the reference program's by a relative error of at most 0.022.
Values may be sent and summed in bfloat16 or wider, within the bound.
A program may use at most 64 MiB of HBM per device.

```python
import math
import jax
import jax.numpy as jnp
from jax import lax

F = 512
TILE = 256
PT = 1
TPD = 24
NODES = 4096
N_ROW = 4
N_COL = 4


def draw_tile_count(key, part):
    key = jax.random.fold_in(key, 11)
    first_key, second_key = jax.random.split(key)
    shifts = jax.random.randint(first_key, (N_ROW, N_COL), 0, 4, dtype=jnp.int32)
    counts = jnp.maximum(2, TPD // jnp.left_shift(jnp.int32(1), shifts))
    chosen = jax.random.randint(second_key, (), 0, N_ROW * N_COL, dtype=jnp.int32)
    flat_counts = counts.reshape(-1).at[chosen].set(TPD)
    return flat_counts.reshape(N_ROW, N_COL).astype(jnp.int32)


def draw_tile_row(key, part):
    key = jax.random.fold_in(key, 23)
    return jax.random.randint(key, (N_ROW, N_COL, TPD), 0, N_COL * PT, dtype=jnp.int32)


def draw_tile_col(key, part):
    key = jax.random.fold_in(key, 37)
    return jax.random.randint(key, (N_ROW, N_COL, TPD), 0, N_ROW * PT, dtype=jnp.int32)


def draw_tile_vals(key, part):
    key = jax.random.fold_in(key, 41)
    mask_key, value_key = jax.random.split(key, 2)
    shape_full = (N_ROW, N_COL, TPD, TILE, TILE)
    spread = 1.0 / math.sqrt(TILE * TPD / 4)
    keeper = jax.random.randint(mask_key, shape_full, 0, 2, dtype=jnp.int32).astype(jnp.float32)
    base = jax.random.normal(value_key, shape_full, jnp.float32)
    base = jnp.clip(base, -3.0, 3.0)
    return (base * keeper * spread).astype(jnp.bfloat16)


def block_levels(stream_key, shape, cuts, low, high):
    factor_of = 1.0
    for axis_at, blocks in cuts:
        heights = jax.random.uniform(jax.random.fold_in(jax.random.fold_in(stream_key, 6), axis_at), (blocks,), jnp.float32, low / len(cuts), high / len(cuts))
        factor_of = factor_of * jnp.repeat(jnp.exp(heights), shape[axis_at] // blocks).reshape((-1,) + (1,) * (len(shape) - 1 - axis_at))
    return factor_of


def noise(rng, dims, scale, bound, cuts=(), kind=jnp.bfloat16):
    array = scale * jax.random.normal(rng, dims, jnp.float32)
    if cuts:
        array = array * block_levels(rng, dims, cuts, -0.22, 0.18)
    return jnp.clip(array, -bound, bound).astype(kind)


def setup_inputs(seed: int = 0) -> dict:
    keys = jax.random.split(jax.random.key(seed), 9)
    return {
        "node_features": noise(keys[0], (NODES, F), 1.0, 6.0, ((0, 16), (1, 2))),
        "weight": noise(keys[1], (F, F), F ** -0.5, 0.25, ((0, 2),)),
        "cotangent": noise(keys[2], (NODES, F), 1.0, 6.0, ((0, 16), (1, 2))),
        "diffusion_time": jnp.clip(jnp.exp(jax.random.uniform(keys[3], (1,), jnp.float32, math.log(0.5), math.log(2.0))), 0.5, 2.0),
        "tile_count": draw_tile_count(jax.random.fold_in(keys[8], 71), 0),
        "tile_row": draw_tile_row(jax.random.fold_in(keys[8], 71), 0),
        "tile_col": draw_tile_col(jax.random.fold_in(keys[8], 71), 0),
        "tile_vals": draw_tile_vals(jax.random.fold_in(keys[8], 71), 0),
    }


def coefficients(diffusion_time):
    elapsed = diffusion_time[0].astype(jnp.float32)
    damping = jnp.exp(-elapsed)
    return (damping, elapsed * damping, elapsed * elapsed * damping * 0.5)

def global_tiles(tile_row, tile_col):
    blocks = N_ROW * N_COL
    block_ids = jnp.arange(blocks, dtype=jnp.int32)
    row_index = block_ids // N_COL
    col_index = block_ids % N_COL
    rows_local = tile_row.reshape(blocks, TPD).astype(jnp.int32)
    cols_local = tile_col.reshape(blocks, TPD).astype(jnp.int32)
    global_rows = row_index[:, None] * (N_COL * PT) + rows_local
    global_cols = (cols_local // PT * N_COL + col_index[:, None]) * PT + cols_local % PT
    return (global_rows.astype(jnp.int32), global_cols.astype(jnp.int32))

def propagate(values, live_slots, source_tiles, target_tiles, source, transpose):
    tile_total = NODES // TILE
    as_tiles = source.astype(jnp.float32).reshape(tile_total, TILE, F)

    def visit(carry, block):
        block_vals, block_live, src_idx, dst_idx = block
        picked = as_tiles[src_idx]
        tiles_f = block_vals.astype(jnp.float32)
        if transpose:
            contrib = jnp.einsum('sik,sih->skh', tiles_f, picked)
        else:
            contrib = jnp.einsum('sik,skh->sih', tiles_f, picked)
        contrib = contrib * block_live[:, None, None]
        return (carry.at[dst_idx].add(contrib), None)
    start = jnp.zeros((tile_total, TILE, F), jnp.float32)
    result, _ = lax.scan(visit, start, (values, live_slots, source_tiles, target_tiles))
    return result.reshape(NODES, F)

def reference(node_features, weight, cotangent, diffusion_time, tile_count, tile_row, tile_col, tile_vals):
    coef_zero, coef_one, coef_two = coefficients(diffusion_time)
    blocks = N_ROW * N_COL
    values = tile_vals.reshape(blocks, TPD, TILE, TILE)
    live_slots = (jnp.arange(TPD, dtype=jnp.int32)[None, :] < tile_count.reshape(blocks, 1)).astype(jnp.float32)
    global_rows, global_cols = global_tiles(tile_row, tile_col)
    first_hop = propagate(values, live_slots, global_cols, global_rows, node_features, False).astype(jnp.bfloat16)
    second_hop = propagate(values, live_slots, global_cols, global_rows, first_hop, False)
    diffused = (coef_zero * node_features.astype(jnp.float32) + coef_one * first_hop.astype(jnp.float32) + coef_two * second_hop).astype(jnp.bfloat16)
    pulled = jnp.dot(cotangent, weight.T, preferred_element_type=jnp.float32).astype(jnp.bfloat16)
    back_one = propagate(values, live_slots, global_rows, global_cols, pulled, True).astype(jnp.bfloat16)
    back_two = propagate(values, live_slots, global_rows, global_cols, back_one, True)
    grad_features = (coef_zero * pulled.astype(jnp.float32) + coef_one * back_one.astype(jnp.float32) + coef_two * back_two).astype(jnp.bfloat16)
    grad_weight = jnp.dot(diffused.T, cotangent, preferred_element_type=jnp.float32) * (1.0 / math.sqrt(NODES))
    return (grad_features, grad_weight)
```

```python
import functools
import math

import jax
import jax.numpy as jnp
from jax import lax
from jax.experimental import pallas as pl
from jax.experimental.pallas import tpu as pltpu
from jax.sharding import PartitionSpec as P

MESH = pl.DeviceIdType.MESH
CHUNKS = 2
F32 = jnp.float32
BF16 = jnp.bfloat16


def build_block(col_tiles, count_ref, rows_ref, cols_ref, vals_ref, a_ref, filled, listed):
    slots, side = vals_ref.shape[0], vals_ref.shape[1]
    places = a_ref.shape[0]
    band = 64

    def clear(p, carry):
        filled[p] = 0
        return carry

    lax.fori_loop(0, places, clear, 0)

    def enter(s, carry):
        place = rows_ref[s] * col_tiles + cols_ref[s]
        at = filled[place]
        listed[place * slots + at] = s
        filled[place] = at + 1
        return carry

    lax.fori_loop(0, jnp.minimum(count_ref[0], slots), enter, 0)

    def add_up(p, carry):
        for b in range(side // band):
            part = pl.ds(b * band, band)

            def more(k, total):
                return total + vals_ref[listed[p * slots + k], part, :].astype(F32)

            total = lax.fori_loop(0, filled[p], more, jnp.zeros((band, side), F32))
            a_ref[p, part, :] = total.astype(BF16)
        return carry

    lax.fori_loop(0, places, add_up, 0)


def hops(
    nrow, ncol, grad_scale,
    t_ref, x_ref, w_ref, g_ref, a_hbm, gf_ref, gw_ref,
    a_ref, xt, source, part, got, own, h_all, gw_part, gw_got, gw_col, gw_sum,
    a_sem, g_s, g_r, p_s, p_r, d_s, d_r, w1_s, w1_r, w2_s, w2_r, w3_s, w3_r,
):
    row, col, depth = lax.axis_index("row"), lax.axis_index("col"), lax.axis_index("depth")
    side = g_ref.shape[0]
    wide = source.shape[3]

    load_a = pltpu.make_async_copy(a_hbm, a_ref, a_sem)
    load_a.start()

    barrier = pltpu.get_barrier_semaphore()
    for i in range(1, nrow):
        pl.semaphore_signal(
            barrier, inc=1, device_id={"row": lax.rem(row + i, nrow)}, device_id_type=MESH)
    for i in range(1, ncol):
        pl.semaphore_signal(
            barrier, inc=1, device_id={"col": lax.rem(col + i, ncol)}, device_id_type=MESH)
    pl.semaphore_signal(barrier, inc=1, device_id={"depth": 1 - depth}, device_id_type=MESH)

    elapsed = t_ref[0]
    damping = jnp.exp(jnp.full((1, side), -elapsed, F32))
    coef_one = elapsed * damping
    coef_two = elapsed * elapsed * damping * 0.5

    flipped = g_ref[...].astype(F32).T.astype(BF16)
    for k in range(CHUNKS):
        source[0, k, col] = flipped[k * wide:(k + 1) * wide, :]
    pl.semaphore_wait(barrier, nrow + ncol - 1)

    def to_col(ref, dst, send, recv, i):
        return pltpu.make_async_remote_copy(
            src_ref=ref, dst_ref=dst, send_sem=send, recv_sem=recv,
            device_id={"col": lax.rem(col + i, ncol)}, device_id_type=MESH)

    def to_row(ref, dst, send, recv, i):
        return pltpu.make_async_remote_copy(
            src_ref=ref, dst_ref=dst, send_sem=send, recv_sem=recv,
            device_id={"row": lax.rem(row + i, nrow)}, device_id_type=MESH)

    def spread(hop, k, i):
        piece = source.at[hop, k, col]
        return to_col(piece, piece, g_s.at[hop, k, i], g_r.at[hop, k, i], i)

    def partial(hop, k, i):
        return to_row(
            part.at[hop, k, lax.rem(row + i, nrow)], got.at[hop, k, row],
            p_s.at[hop, k, i], p_r.at[hop, k, i], i)

    def swap(k):
        piece = h_all.at[k, depth]
        return pltpu.make_async_remote_copy(
            src_ref=piece, dst_ref=piece, send_sem=d_s.at[k], recv_sem=d_r.at[k],
            device_id={"depth": 1 - depth}, device_id_type=MESH)

    def gw_rows(k, i):
        return to_row(
            gw_part.at[k, lax.rem(row + i, nrow)], gw_got.at[k, row],
            w1_s.at[k, i], w1_r.at[k, i], i)

    def gw_cols(k, i):
        piece = gw_col.at[k, col]
        return to_col(piece, piece, w2_s.at[k, i], w2_r.at[k, i], i)

    def gw_back(k, i):
        piece = gw_sum.at[k, row]
        return to_row(piece, piece, w3_s.at[k, i], w3_r.at[k, i], i)

    def start_all(copy, n):
        for i in range(1, n):
            copy(i).start()

    def recv_all(copy, n):
        for i in range(1, n):
            copy(i).wait_recv()

    def multiply(hop, k):
        recv_all(functools.partial(spread, hop, k), ncol)

        def target(i, carry):
            goal = lax.rem(row + i, nrow)
            total = jnp.zeros((wide, side), F32)
            for j in range(ncol):
                total += jnp.dot(
                    source[hop, k, j], a_ref[j * nrow + goal], preferred_element_type=F32)

            @pl.when(i < nrow)
            def _():
                part[hop, k, goal] = total.astype(BF16)
                partial(hop, k, i).start()

            @pl.when(i == nrow)
            def _():
                own[k] = total
            return carry

        lax.fori_loop(1, nrow + 1, target, 0)

    def collect(hop, k):
        recv_all(functools.partial(partial, hop, k), nrow)
        total = own[k]
        for i in range(1, nrow):
            total += got[hop, k, lax.rem(row + i, nrow)].astype(F32)
        return total

    for k in range(CHUNKS):
        start_all(functools.partial(spread, 0, k), ncol)
    xt[...] = x_ref[...].astype(F32).T.astype(BF16)
    load_a.wait()
    for k in range(CHUNKS):
        multiply(0, k)
    for k in range(CHUNKS):
        source[1, k, col] = collect(0, k).astype(BF16)
        start_all(functools.partial(spread, 1, k), ncol)
    for k in range(CHUNKS):
        multiply(1, k)
    for k in range(CHUNKS):
        total = (
            damping * source[0, k, col].astype(F32)
            + coef_one * source[1, k, col].astype(F32)
            + coef_two * collect(1, k))
        h_all[k, depth] = total.T.astype(BF16)
        swap(k).start()
    grad = jnp.zeros((side, side), F32)
    for k in range(CHUNKS):
        swap(k).wait_recv()
        for d in range(2):
            terms = jnp.dot(xt[...], h_all[k, d], preferred_element_type=F32) * grad_scale
            gw_part[k, :, :, d * wide:(d + 1) * wide] = terms.astype(BF16).reshape(
                nrow, side // nrow, wide)
        start_all(functools.partial(gw_rows, k), nrow)
    for k in range(CHUNKS):
        for d in range(2):
            at = (d * CHUNKS + k) * wide
            grad += lax.dot_general(
                h_all[k, d], w_ref[:, at:at + wide], (((1,), (1,)), ((), ())),
                preferred_element_type=F32)
    gf_ref[...] = grad.astype(BF16)
    for k in range(CHUNKS):
        recv_all(functools.partial(gw_rows, k), nrow)
        total = gw_part[k, row].astype(F32)
        for i in range(1, nrow):
            total += gw_got[k, lax.rem(row + i, nrow)].astype(F32)
        gw_col[k, col] = total.astype(BF16)
        start_all(functools.partial(gw_cols, k), ncol)
    for k in range(CHUNKS):
        recv_all(functools.partial(gw_cols, k), ncol)
        total = gw_col[k, 0].astype(F32)
        for j in range(1, ncol):
            total += gw_col[k, j].astype(F32)
        gw_sum[k, row] = total.astype(BF16)
        start_all(functools.partial(gw_back, k), nrow)
    for k in range(CHUNKS):
        recv_all(functools.partial(gw_back, k), nrow)
        for d in range(2):
            at = (d * CHUNKS + k) * wide
            gw_ref[:, at:at + wide] = gw_sum[k, :, :, d * wide:(d + 1) * wide].reshape(side, wide)

    for k in range(CHUNKS):
        for hop in range(2):
            for i in range(1, ncol):
                spread(hop, k, i).wait_send()
            for i in range(1, nrow):
                partial(hop, k, i).wait_send()
        swap(k).wait_send()
        for i in range(1, nrow):
            gw_rows(k, i).wait_send()
            gw_back(k, i).wait_send()
        for i in range(1, ncol):
            gw_cols(k, i).wait_send()


def per_device(
    node_features, weight, cotangent, diffusion_time, tile_count, tile_row, tile_col, tile_vals
):
    nrow, ncol = lax.axis_size("row"), lax.axis_size("col")
    values = tile_vals[0, 0]
    slots, side = values.shape[0], values.shape[-1]
    features = weight.shape[1]
    half = cotangent.shape[1]
    wide = half // CHUNKS
    places = nrow * ncol
    vmem = pl.BlockSpec(memory_space=pltpu.VMEM)
    smem = pl.BlockSpec(memory_space=pltpu.SMEM)

    block = pl.pallas_call(
        functools.partial(build_block, nrow),
        out_shape=jax.ShapeDtypeStruct((places, side, side), BF16),
        in_specs=[smem, smem, smem, vmem],
        out_specs=vmem,
        scratch_shapes=[
            pltpu.SMEM((places,), jnp.int32),
            pltpu.SMEM((places * slots,), jnp.int32),
        ],
        compiler_params=pltpu.CompilerParams(vmem_limit_bytes=32 << 20),
    )(tile_count.reshape(1), tile_row.reshape(slots), tile_col.reshape(slots), values)

    dma = pltpu.SemaphoreType.DMA
    grad_features, grad_weight = pl.pallas_call(
        functools.partial(hops, nrow, ncol, 1.0 / math.sqrt(side * places)),
        out_shape=(
            jax.ShapeDtypeStruct((side, half), BF16),
            jax.ShapeDtypeStruct((half, features), BF16),
        ),
        in_specs=[smem, vmem, vmem, vmem, pl.BlockSpec(memory_space=pl.ANY)],
        out_specs=(vmem, vmem),
        scratch_shapes=[
            pltpu.VMEM((places, side, side), BF16),
            pltpu.VMEM((half, side), BF16),
            pltpu.VMEM((2, CHUNKS, ncol, wide, side), BF16),
            pltpu.VMEM((2, CHUNKS, nrow, wide, side), BF16),
            pltpu.VMEM((2, CHUNKS, nrow, wide, side), BF16),
            pltpu.VMEM((CHUNKS, wide, side), F32),
            pltpu.VMEM((CHUNKS, 2, side, wide), BF16),
            pltpu.VMEM((CHUNKS, nrow, half // nrow, 2 * wide), BF16),
            pltpu.VMEM((CHUNKS, nrow, half // nrow, 2 * wide), BF16),
            pltpu.VMEM((CHUNKS, ncol, half // nrow, 2 * wide), BF16),
            pltpu.VMEM((CHUNKS, nrow, half // nrow, 2 * wide), BF16),
            dma,
            dma((2, CHUNKS, ncol)), dma((2, CHUNKS, ncol)),
            dma((2, CHUNKS, nrow)), dma((2, CHUNKS, nrow)),
            dma((CHUNKS,)), dma((CHUNKS,)),
            dma((CHUNKS, nrow)), dma((CHUNKS, nrow)),
            dma((CHUNKS, ncol)), dma((CHUNKS, ncol)),
            dma((CHUNKS, nrow)), dma((CHUNKS, nrow)),
        ],
        compiler_params=pltpu.CompilerParams(
            collective_id=0, has_side_effects=True, vmem_limit_bytes=40 << 20),
    )(diffusion_time, node_features, weight, cotangent, block)
    return (grad_features, grad_weight.astype(F32))


def solution(mesh):
    return jax.shard_map(
        per_device,
        mesh=mesh,
        in_specs=(
            P(("row", "col"), "depth"),
            P("depth", None),
            P(("row", "col"), "depth"),
            P(),
            P("row", "col"),
            P("row", "col", None),
            P("row", "col", None),
            P("row", "col", None, None, None),
        ),
        out_specs=(P(("row", "col"), "depth"), P("depth", None)),
        check_vma=False,
    )
```

```python
import functools
import math

import jax
import jax.numpy as jnp
from jax import lax
from jax.experimental import pallas as pl
from jax.experimental.pallas import tpu as pltpu
from jax.sharding import PartitionSpec as P

MESH = pl.DeviceIdType.MESH
CHUNKS = 2
F32 = jnp.float32
BF16 = jnp.bfloat16


def hops(
    nrow, ncol, grad_scale,
    t_hbm, x_hbm, w_hbm, g_hbm, count_hbm, rows_hbm, cols_hbm, vals_hbm, gf_ref, gw_ref,
    t_ref, x_ref, w_ref, g_ref, count_ref, rows_ref, cols_ref, vals_ref,
    placed, rank, order, placed_at, tile_at, running, tiles,
    xt, source, total, part, got, h_all, gw_part, gw_got, gw_col, gw_back_to, gw_sum,
    load, g_s, g_r, p_s, p_r, d_s, d_r, w1_s, w1_r, w2_s, w2_r, w3_s, w3_r, w4_s, w4_r,
):
    row, col, depth = lax.axis_index("row"), lax.axis_index("col"), lax.axis_index("depth")
    side = g_ref.shape[0]
    slots = vals_ref.shape[0]
    wide = source.shape[3]
    places = nrow * ncol
    split = gw_col.shape[2] < gw_part.shape[2]

    loads = [
        pltpu.make_async_copy(src, dst, load.at[n])
        for n, (src, dst) in enumerate((
            (g_hbm, g_ref), (rows_hbm, rows_ref), (cols_hbm, cols_ref), (count_hbm, count_ref),
            (t_hbm, t_ref), (vals_hbm, vals_ref), (x_hbm, x_ref), (w_hbm, w_ref)))
    ]
    for copy in loads:
        copy.start()

    barrier = pltpu.get_barrier_semaphore()
    for i in range(1, nrow):
        pl.semaphore_signal(
            barrier, inc=1, device_id={"row": lax.rem(row + i, nrow)}, device_id_type=MESH)
    for i in range(1, ncol):
        pl.semaphore_signal(
            barrier, inc=1, device_id={"col": lax.rem(col + i, ncol)}, device_id_type=MESH)
    pl.semaphore_signal(barrier, inc=1, device_id={"depth": 1 - depth}, device_id_type=MESH)

    loads[0].wait()
    flipped = g_ref[...].astype(F32).T.astype(BF16)
    for k in range(CHUNKS):
        source[0, k, col] = flipped[k * wide:(k + 1) * wide, :]
    pl.semaphore_wait(barrier, nrow + ncol - 1)

    def to_col(ref, dst, send, recv, i):
        return pltpu.make_async_remote_copy(
            src_ref=ref, dst_ref=dst, send_sem=send, recv_sem=recv,
            device_id={"col": lax.rem(col + i, ncol)}, device_id_type=MESH)

    def to_row(ref, dst, send, recv, i):
        return pltpu.make_async_remote_copy(
            src_ref=ref, dst_ref=dst, send_sem=send, recv_sem=recv,
            device_id={"row": lax.rem(row + i, nrow)}, device_id_type=MESH)

    def pass_on(hop, k, p, up):
        piece = source.at[hop, k, p]
        return pltpu.make_async_remote_copy(
            src_ref=piece, dst_ref=piece, send_sem=g_s.at[hop, k, up, p],
            recv_sem=g_r.at[hop, k, p],
            device_id={"col": jnp.minimum(col + 1, ncol - 1) if up else jnp.maximum(col - 1, 0)},
            device_id_type=MESH)

    def partial(hop, k, i):
        return to_row(
            part.at[hop, k, lax.rem(row + i, nrow)], got.at[hop, k, row],
            p_s.at[hop, k, i], p_r.at[hop, k, i], i)

    def swap(k):
        piece = h_all.at[k, depth]
        return pltpu.make_async_remote_copy(
            src_ref=piece, dst_ref=piece, send_sem=d_s.at[k], recv_sem=d_r.at[k],
            device_id={"depth": 1 - depth}, device_id_type=MESH)

    def gw_rows(k, i):
        return to_row(
            gw_part.at[k, lax.rem(row + i, nrow)], gw_got.at[k, row],
            w1_s.at[k, i], w1_r.at[k, i], i)

    def gw_cols(k, i):
        mine = gw_back_to.at[k, lax.rem(col + i, ncol)] if split else gw_col.at[k, col]
        return to_col(mine, gw_col.at[k, col], w2_s.at[k, i], w2_r.at[k, i], i)

    def gw_share(k, i):
        piece = gw_sum.at[k, row, col]
        return to_col(piece, piece, w4_s.at[k, i], w4_r.at[k, i], i)

    def gw_back(k, i):
        piece = gw_sum.at[k, row]
        return to_row(piece, piece, w3_s.at[k, i], w3_r.at[k, i], i)

    def start_all(copy, n):
        for i in range(1, n):
            copy(i).start()

    def recv_all(copy, n):
        for i in range(1, n):
            copy(i).wait_recv()

    def spread(hop, k):
        @pl.when(col < ncol - 1)
        def _():
            pass_on(hop, k, col, 1).start()

        @pl.when(col > 0)
        def _():
            pass_on(hop, k, col, 0).start()

    def relay(hop, k, s):
        @pl.when(col >= s)
        def _():
            pass_on(hop, k, col - s, 1).wait_recv()

            @pl.when(col < ncol - 1)
            def _():
                pass_on(hop, k, col - s, 1).start()

        @pl.when(col + s < ncol)
        def _():
            pass_on(hop, k, col + s, 0).wait_recv()

            @pl.when(col > 0)
            def _():
                pass_on(hop, k, col + s, 0).start()

    def add_piece(hop, k, p, first):
        def target(goal, carry):
            term = jnp.dot(
                source[hop, k, p], tiles[tile_at[p * nrow + goal]], preferred_element_type=F32)
            if first:
                total[k, goal] = term
            else:
                total[k, goal] += term
            return carry

        lax.fori_loop(0, nrow, target, 0, unroll=nrow <= 4)

    def add_arrived(hop, k, s):
        @pl.when(col >= s)
        def _():
            add_piece(hop, k, col - s, False)

        @pl.when(col + s < ncol)
        def _():
            add_piece(hop, k, col + s, False)

    def hand_out(hop, k):
        for i in range(1, nrow):
            goal = lax.rem(row + i, nrow)
            part[hop, k, goal] = total[k, goal].astype(BF16)
            partial(hop, k, i).start()

    def collect(hop, k):
        recv_all(functools.partial(partial, hop, k), nrow)
        terms = total[k, row]
        for i in range(1, nrow):
            terms += got[hop, k, lax.rem(row + i, nrow)].astype(F32)
        return terms

    def relay_all(hop, s):
        for k in range(CHUNKS):
            relay(hop, k, s)

    for k in range(CHUNKS):
        spread(0, k)

    for copy in loads[1:4]:
        copy.wait()
    live = count_ref[0]

    def enter(s, carry):
        placed[s] = jnp.where(s < live, rows_ref[s] * nrow + cols_ref[s], places)
        return carry

    lax.fori_loop(0, slots, enter, 0)

    def count_before(s, carry):
        mine = placed[s]
        before = jnp.int32(0)
        for other in range(slots):
            theirs = placed[other]
            ahead = (theirs < mine) | ((theirs == mine) & (other < s))
            before += jnp.where(ahead, 1, 0)
        rank[s] = before
        return carry

    lax.fori_loop(0, slots, count_before, 0)

    def invert(n, carry):
        slot, place = jnp.int32(0), jnp.int32(0)
        for s in range(slots):
            here = rank[s] == n
            slot += jnp.where(here, s, 0)
            place += jnp.where(here, placed[s], 0)
        order[n] = slot
        placed_at[n] = place
        return carry

    lax.fori_loop(0, slots, invert, 0)

    def find(p, carry):
        last, held = jnp.int32(-1), jnp.int32(0)
        for s in range(slots):
            last += jnp.where(placed[s] <= p, 1, 0)
            held += jnp.where(placed[s] == p, 1, 0)
        tile_at[p] = jnp.where(held > 0, last, slots)
        return carry

    lax.fori_loop(0, places, find, 0)
    relay_all(0, 1)
    loads[5].wait()
    running[...] = jnp.zeros_like(running)
    tiles[slots] = jnp.zeros((side, side), BF16)

    def add_up(n, carry):
        slot = order[n]
        same = placed_at[n] == placed_at[jnp.maximum(n - 1, 0)]
        keep = jnp.where(same, 1.0, 0.0).astype(F32)
        for b in range(0, side, 64):
            band = pl.ds(b, 64)
            now = running[band, :] * keep + vals_ref[slot, band, :].astype(F32)
            running[band, :] = now
            tiles[n, band, :] = now.astype(BF16)
        return carry

    for s in range(1, ncol):
        if s > 1:
            relay_all(0, s)
        if s < ncol - 1:
            steps = ncol - 2
            lax.fori_loop(slots * (s - 1) // steps, slots * s // steps, add_up, 0)
    loads[6].wait()
    xt[...] = x_ref[...].astype(F32).T.astype(BF16)
    for k in range(CHUNKS):
        for s in range(ncol):
            if s == 0:
                add_piece(0, k, col, True)
            else:
                add_arrived(0, k, s)
        hand_out(0, k)
    for k in range(CHUNKS):
        source[1, k, col] = collect(0, k).astype(BF16)
        spread(1, k)
    for s in range(ncol):
        for k in range(CHUNKS):
            if s > 0:
                relay(1, k, s)
                add_arrived(1, k, s)
            else:
                add_piece(1, k, col, True)
            if s == ncol - 1:
                hand_out(1, k)

    loads[4].wait()
    elapsed = t_ref[0]
    damping = jnp.exp(jnp.full((1, side), -elapsed, F32))
    coef_one = elapsed * damping
    coef_two = elapsed * elapsed * damping * 0.5
    for k in range(CHUNKS):
        terms = (
            damping * source[0, k, col].astype(F32)
            + coef_one * source[1, k, col].astype(F32)
            + coef_two * collect(1, k))
        h_all[k, depth] = terms.T.astype(BF16)
        swap(k).start()
    loads[7].wait()
    for k in range(CHUNKS):
        swap(k).wait_recv()
        for d in range(2):
            terms = jnp.dot(xt[...], h_all[k, d], preferred_element_type=F32) * grad_scale
            gw_part[k, :, :, d * wide:(d + 1) * wide] = terms.astype(BF16).reshape(
                nrow, side // nrow, wide)
        start_all(functools.partial(gw_rows, k), nrow)
    grad = jnp.zeros((side, side), F32)
    for k in range(CHUNKS):
        for d in range(2):
            at = (d * CHUNKS + k) * wide
            grad += lax.dot_general(
                h_all[k, d], w_ref[:, at:at + wide], (((1,), (1,)), ((), ())),
                preferred_element_type=F32)
    gf_ref[...] = grad.astype(BF16)
    for k in range(CHUNKS):
        recv_all(functools.partial(gw_rows, k), nrow)
        terms = gw_part[k, row].astype(F32)
        for i in range(1, nrow):
            terms += gw_got[k, lax.rem(row + i, nrow)].astype(F32)
        if split:
            gw_back_to[k] = terms.astype(BF16).reshape(gw_back_to.shape[1:])
            gw_col[k, col] = gw_back_to[k, col]
        else:
            gw_col[k, col] = terms.astype(BF16)
        start_all(functools.partial(gw_cols, k), ncol)
    for k in range(CHUNKS):
        recv_all(functools.partial(gw_cols, k), ncol)
        terms = gw_col[k, 0].astype(F32)
        for j in range(1, ncol):
            terms += gw_col[k, j].astype(F32)
        if split:
            gw_sum[k, row, col] = terms.astype(BF16)
            start_all(functools.partial(gw_share, k), ncol)
        else:
            gw_sum[k, row, 0] = terms.astype(BF16)
            start_all(functools.partial(gw_back, k), nrow)
    if split:
        for k in range(CHUNKS):
            recv_all(functools.partial(gw_share, k), ncol)
            start_all(functools.partial(gw_back, k), nrow)
    for k in range(CHUNKS):
        recv_all(functools.partial(gw_back, k), nrow)
        for d in range(2):
            at = (d * CHUNKS + k) * wide
            gw_ref[:, at:at + wide] = gw_sum[k, :, :, :, d * wide:(d + 1) * wide].reshape(
                side, wide)

    for k in range(CHUNKS):
        for hop in range(2):
            for p in range(ncol):
                @pl.when((p <= col) & (col < ncol - 1))
                def _():
                    pass_on(hop, k, p, 1).wait_send()

                @pl.when((p >= col) & (col > 0))
                def _():
                    pass_on(hop, k, p, 0).wait_send()
            for i in range(1, nrow):
                partial(hop, k, i).wait_send()
        swap(k).wait_send()
        for i in range(1, nrow):
            gw_rows(k, i).wait_send()
            gw_back(k, i).wait_send()
        for i in range(1, ncol):
            gw_cols(k, i).wait_send()
            if split:
                gw_share(k, i).wait_send()


def per_device(
    node_features, weight, cotangent, diffusion_time, tile_count, tile_row, tile_col, tile_vals
):
    nrow, ncol = lax.axis_size("row"), lax.axis_size("col")
    values = tile_vals[0, 0]
    slots, side = values.shape[0], values.shape[-1]
    features = weight.shape[1]
    half = cotangent.shape[1]
    wide = half // CHUNKS
    places = nrow * ncol
    vmem = pl.BlockSpec(memory_space=pltpu.VMEM)

    dma = pltpu.SemaphoreType.DMA
    hbm = pl.BlockSpec(memory_space=pltpu.HBM)
    held = half // nrow
    piece = held // ncol if (held // ncol) % 16 == 0 else held
    grad_features, grad_weight = pl.pallas_call(
        functools.partial(hops, nrow, ncol, 1.0 / math.sqrt(side * places)),
        out_shape=(
            jax.ShapeDtypeStruct((side, half), BF16),
            jax.ShapeDtypeStruct((half, features), BF16),
        ),
        in_specs=[hbm] * 8,
        out_specs=(vmem, vmem),
        scratch_shapes=[
            pltpu.SMEM((1,), F32),
            pltpu.VMEM((side, half), BF16),
            pltpu.VMEM((half, features), BF16),
            pltpu.VMEM((side, half), BF16),
            pltpu.SMEM((1,), jnp.int32),
            pltpu.SMEM((slots,), jnp.int32),
            pltpu.SMEM((slots,), jnp.int32),
            pltpu.VMEM((slots, side, side), BF16),
            pltpu.SMEM((slots,), jnp.int32),
            pltpu.SMEM((slots,), jnp.int32),
            pltpu.SMEM((slots,), jnp.int32),
            pltpu.SMEM((slots,), jnp.int32),
            pltpu.SMEM((places,), jnp.int32),
            pltpu.VMEM((side, side), F32),
            pltpu.VMEM((slots + 1, side, side), BF16),
            pltpu.VMEM((half, side), BF16),
            pltpu.VMEM((2, CHUNKS, ncol, wide, side), BF16),
            pltpu.VMEM((CHUNKS, nrow, wide, side), F32),
            pltpu.VMEM((2, CHUNKS, nrow, wide, side), BF16),
            pltpu.VMEM((2, CHUNKS, nrow, wide, side), BF16),
            pltpu.VMEM((CHUNKS, 2, side, wide), BF16),
            pltpu.VMEM((CHUNKS, nrow, held, 2 * wide), BF16),
            pltpu.VMEM((CHUNKS, nrow, held, 2 * wide), BF16),
            pltpu.VMEM((CHUNKS, ncol, piece, 2 * wide), BF16),
            pltpu.VMEM((CHUNKS, held // piece, piece, 2 * wide), BF16),
            pltpu.VMEM((CHUNKS, nrow, held // piece, piece, 2 * wide), BF16),
            dma((8,)),
            dma((2, CHUNKS, 2, ncol)), dma((2, CHUNKS, ncol)),
            dma((2, CHUNKS, nrow)), dma((2, CHUNKS, nrow)),
            dma((CHUNKS,)), dma((CHUNKS,)),
            dma((CHUNKS, nrow)), dma((CHUNKS, nrow)),
            dma((CHUNKS, ncol)), dma((CHUNKS, ncol)),
            dma((CHUNKS, nrow)), dma((CHUNKS, nrow)),
            dma((CHUNKS, ncol)), dma((CHUNKS, ncol)),
        ],
        compiler_params=pltpu.CompilerParams(
            collective_id=0, has_side_effects=True, vmem_limit_bytes=56 << 20),
    )(
        diffusion_time, node_features, weight, cotangent, tile_count.reshape(1),
        tile_row.reshape(slots), tile_col.reshape(slots), values)
    return (grad_features, grad_weight.astype(F32))


def solution(mesh):
    return jax.shard_map(
        per_device,
        mesh=mesh,
        in_specs=(
            P(("row", "col"), "depth"),
            P("depth", None),
            P(("row", "col"), "depth"),
            P(),
            P("row", "col"),
            P("row", "col", None),
            P("row", "col", None),
            P("row", "col", None, None, None),
        ),
        out_specs=(P(("row", "col"), "depth"), P("depth", None)),
        check_vma=False,
    )
```

```python
import functools
import math

import jax
import jax.numpy as jnp
from jax import lax
from jax.experimental import pallas as pl
from jax.experimental.pallas import tpu as pltpu
from jax.sharding import PartitionSpec as P

MESH = pl.DeviceIdType.MESH
CHUNKS = 2
F32 = jnp.float32
BF16 = jnp.bfloat16


def hops(
    nrow, ncol, grad_scale,
    t_hbm, x_hbm, w_hbm, g_hbm, count_hbm, rows_hbm, cols_hbm, vals_hbm, gf_ref, gw_ref,
    t_ref, x_ref, w_ref, g_ref, count_ref, rows_ref, cols_ref, vals_ref,
    placed, rank, order, placed_at, tile_at, running, tiles,
    xt, source, total, part, got, h_all, gw_part, gw_got, gw_col, gw_back_to, gw_sum,
    load, g_s, g_r, p_s, p_r, d_s, d_r, w1_s, w1_r, w2_s, w2_r, w3_s, w3_r, w4_s, w4_r,
):
    row, col, depth = lax.axis_index("row"), lax.axis_index("col"), lax.axis_index("depth")
    side = g_ref.shape[0]
    slots = vals_ref.shape[0]
    wide = source.shape[3]
    places = nrow * ncol
    split = gw_col.shape[2] < gw_part.shape[2]

    loads = [
        pltpu.make_async_copy(src, dst, load.at[n])
        for n, (src, dst) in enumerate((
            (g_hbm, g_ref), (rows_hbm, rows_ref), (cols_hbm, cols_ref), (count_hbm, count_ref),
            (t_hbm, t_ref), (vals_hbm, vals_ref), (x_hbm, x_ref), (w_hbm, w_ref)))
    ]
    for copy in loads:
        copy.start()

    barrier = pltpu.get_barrier_semaphore()
    for i in range(1, nrow):
        pl.semaphore_signal(
            barrier, inc=1, device_id={"row": lax.rem(row + i, nrow)}, device_id_type=MESH)
    for i in range(1, ncol):
        pl.semaphore_signal(
            barrier, inc=1, device_id={"col": lax.rem(col + i, ncol)}, device_id_type=MESH)
    pl.semaphore_signal(barrier, inc=1, device_id={"depth": 1 - depth}, device_id_type=MESH)

    loads[0].wait()
    flipped = g_ref[...].astype(F32).T.astype(BF16)
    for k in range(CHUNKS):
        source[0, k, col] = flipped[k * wide:(k + 1) * wide, :]
    pl.semaphore_wait(barrier, nrow + ncol - 1)

    def to_col(ref, dst, send, recv, i):
        return pltpu.make_async_remote_copy(
            src_ref=ref, dst_ref=dst, send_sem=send, recv_sem=recv,
            device_id={"col": lax.rem(col + i, ncol)}, device_id_type=MESH)

    def to_row(ref, dst, send, recv, i):
        return pltpu.make_async_remote_copy(
            src_ref=ref, dst_ref=dst, send_sem=send, recv_sem=recv,
            device_id={"row": lax.rem(row + i, nrow)}, device_id_type=MESH)

    def spread(hop, k, i):
        piece = source.at[hop, k, col]
        return to_col(piece, piece, g_s.at[hop, k, i], g_r.at[hop, k, i], i)

    def partial(hop, k, i):
        return to_row(
            part.at[hop, k, lax.rem(row + i, nrow)], got.at[hop, k, row],
            p_s.at[hop, k, i], p_r.at[hop, k, i], i)

    def swap(k):
        piece = h_all.at[k, depth]
        return pltpu.make_async_remote_copy(
            src_ref=piece, dst_ref=piece, send_sem=d_s.at[k], recv_sem=d_r.at[k],
            device_id={"depth": 1 - depth}, device_id_type=MESH)

    def gw_rows(k, i):
        return to_row(
            gw_part.at[k, lax.rem(row + i, nrow)], gw_got.at[k, row],
            w1_s.at[k, i], w1_r.at[k, i], i)

    def gw_cols(k, i):
        mine = gw_back_to.at[k, lax.rem(col + i, ncol)] if split else gw_col.at[k, col]
        return to_col(mine, gw_col.at[k, col], w2_s.at[k, i], w2_r.at[k, i], i)

    def gw_share(k, i):
        piece = gw_sum.at[k, row, col]
        return to_col(piece, piece, w4_s.at[k, i], w4_r.at[k, i], i)

    def gw_back(k, i):
        piece = gw_sum.at[k, row]
        return to_row(piece, piece, w3_s.at[k, i], w3_r.at[k, i], i)

    def start_all(copy, n):
        for i in range(1, n):
            copy(i).start()

    def recv_all(copy, n):
        for i in range(1, n):
            copy(i).wait_recv()

    def sent_all(copy, n):
        for i in range(1, n):
            copy(i).wait_send()

    def multiply(hop, k):
        recv_all(functools.partial(spread, hop, k), ncol)

        def target(i, carry):
            goal = lax.rem(row + i, nrow)
            terms = jnp.zeros((wide, side), F32)
            for p in range(ncol):
                terms += jnp.dot(
                    source[hop, k, p], tiles[tile_at[p * nrow + goal]],
                    preferred_element_type=F32)

            @pl.when(i < nrow)
            def _():
                part[hop, k, goal] = terms.astype(BF16)
                partial(hop, k, i).start()

            @pl.when(i == nrow)
            def _():
                total[k] = terms
            return carry

        lax.fori_loop(1, nrow + 1, target, 0)

    def collect(hop, k):
        recv_all(functools.partial(partial, hop, k), nrow)
        terms = total[k]
        for i in range(1, nrow):
            terms += got[hop, k, lax.rem(row + i, nrow)].astype(F32)
        return terms

    def spread_all(hop, k):
        if k > 0:
            sent_all(functools.partial(spread, hop, k - 1), ncol)
        start_all(functools.partial(spread, hop, k), ncol)

    spread_all(0, 0)

    for copy in loads[1:4]:
        copy.wait()
    live = count_ref[0]

    def enter(s, carry):
        placed[s] = jnp.where(s < live, rows_ref[s] * nrow + cols_ref[s], places)
        return carry

    lax.fori_loop(0, slots, enter, 0)

    def count_before(s, carry):
        mine = placed[s]
        before = jnp.int32(0)
        for other in range(slots):
            theirs = placed[other]
            ahead = (theirs < mine) | ((theirs == mine) & (other < s))
            before += jnp.where(ahead, 1, 0)
        rank[s] = before
        return carry

    lax.fori_loop(0, slots, count_before, 0)

    def invert(n, carry):
        slot, place = jnp.int32(0), jnp.int32(0)
        for s in range(slots):
            here = rank[s] == n
            slot += jnp.where(here, s, 0)
            place += jnp.where(here, placed[s], 0)
        order[n] = slot
        placed_at[n] = place
        return carry

    lax.fori_loop(0, slots, invert, 0)

    def find(p, carry):
        last, held = jnp.int32(-1), jnp.int32(0)
        for s in range(slots):
            last += jnp.where(placed[s] <= p, 1, 0)
            held += jnp.where(placed[s] == p, 1, 0)
        tile_at[p] = jnp.where(held > 0, last, slots)
        return carry

    lax.fori_loop(0, places, find, 0)
    loads[5].wait()
    running[...] = jnp.zeros_like(running)
    tiles[slots] = jnp.zeros((side, side), BF16)

    def add_up(n, carry):
        slot = order[n]
        same = placed_at[n] == placed_at[jnp.maximum(n - 1, 0)]
        keep = jnp.where(same, 1.0, 0.0).astype(F32)
        for b in range(0, side, 64):
            band = pl.ds(b, 64)
            now = running[band, :] * keep + vals_ref[slot, band, :].astype(F32)
            running[band, :] = now
            tiles[n, band, :] = now.astype(BF16)
        return carry

    lax.fori_loop(0, slots // 2, add_up, 0)
    for k in range(1, CHUNKS):
        spread_all(0, k)
    lax.fori_loop(slots // 2, slots, add_up, 0)
    for copy in loads[4:5] + loads[6:]:
        copy.wait()
    xt[...] = x_ref[...].astype(F32).T.astype(BF16)
    elapsed = t_ref[0]
    damping = jnp.exp(jnp.full((1, side), -elapsed, F32))
    coef_one = elapsed * damping
    coef_two = elapsed * elapsed * damping * 0.5

    def turn(k):
        source[1, k, col] = collect(0, k).astype(BF16)
        spread_all(1, k)

    def join(k):
        terms = (
            damping * source[0, k, col].astype(F32)
            + coef_one * source[1, k, col].astype(F32)
            + coef_two * collect(1, k))
        h_all[k, depth] = terms.T.astype(BF16)
        swap(k).start()

    def gw_begin(k):
        swap(k).wait_recv()
        for d in range(2):
            terms = jnp.dot(xt[...], h_all[k, d], preferred_element_type=F32) * grad_scale
            gw_part[k, :, :, d * wide:(d + 1) * wide] = terms.astype(BF16).reshape(
                nrow, side // nrow, wide)
        start_all(functools.partial(gw_rows, k), nrow)

    def gw_over_rows(k):
        recv_all(functools.partial(gw_rows, k), nrow)
        terms = gw_part[k, row].astype(F32)
        for i in range(1, nrow):
            terms += gw_got[k, lax.rem(row + i, nrow)].astype(F32)
        if split:
            gw_back_to[k] = terms.astype(BF16).reshape(gw_back_to.shape[1:])
            gw_col[k, col] = gw_back_to[k, col]
        else:
            gw_col[k, col] = terms.astype(BF16)
        start_all(functools.partial(gw_cols, k), ncol)

    def gw_over_cols(k):
        recv_all(functools.partial(gw_cols, k), ncol)
        terms = gw_col[k, 0].astype(F32)
        for j in range(1, ncol):
            terms += gw_col[k, j].astype(F32)
        if split:
            gw_sum[k, row, col] = terms.astype(BF16)
            start_all(functools.partial(gw_share, k), ncol)
        else:
            gw_sum[k, row, 0] = terms.astype(BF16)

    def gw_return(k):
        if split:
            recv_all(functools.partial(gw_share, k), ncol)
        start_all(functools.partial(gw_back, k), nrow)

    def gw_end(k):
        recv_all(functools.partial(gw_back, k), nrow)
        for d in range(2):
            at = (d * CHUNKS + k) * wide
            gw_ref[:, at:at + wide] = gw_sum[k, :, :, :, d * wide:(d + 1) * wide].reshape(
                side, wide)

    multiply(0, 0)
    turn(0)
    multiply(0, 1)
    turn(1)
    multiply(1, 0)
    join(0)
    multiply(1, 1)
    gw_begin(0)
    join(1)
    gw_over_rows(0)
    gw_begin(1)
    grad = jnp.zeros((side, side), F32)
    for k in range(CHUNKS):
        for d in range(2):
            at = (d * CHUNKS + k) * wide
            grad += lax.dot_general(
                h_all[k, d], w_ref[:, at:at + wide], (((1,), (1,)), ((), ())),
                preferred_element_type=F32)
    gf_ref[...] = grad.astype(BF16)
    gw_over_cols(0)
    gw_over_rows(1)
    gw_return(0)
    gw_over_cols(1)
    gw_return(1)
    for k in range(CHUNKS):
        gw_end(k)

    for k in range(CHUNKS):
        for hop in range(2):
            if k == CHUNKS - 1:
                sent_all(functools.partial(spread, hop, k), ncol)
            sent_all(functools.partial(partial, hop, k), nrow)
        swap(k).wait_send()
        for i in range(1, nrow):
            gw_rows(k, i).wait_send()
            gw_back(k, i).wait_send()
        for i in range(1, ncol):
            gw_cols(k, i).wait_send()
            if split:
                gw_share(k, i).wait_send()


def emit(gf_in, gw_in, gf_ref, gw_ref):
    gf_ref[...] = gf_in[...]
    gw_ref[...] = gw_in[...].astype(F32)


def per_device(
    node_features, weight, cotangent, diffusion_time, tile_count, tile_row, tile_col, tile_vals
):
    nrow, ncol = lax.axis_size("row"), lax.axis_size("col")
    values = tile_vals[0, 0]
    slots, side = values.shape[0], values.shape[-1]
    features = weight.shape[1]
    half = cotangent.shape[1]
    wide = half // CHUNKS
    places = nrow * ncol
    vmem = pl.BlockSpec(memory_space=pltpu.VMEM)

    dma = pltpu.SemaphoreType.DMA
    hbm = pl.BlockSpec(memory_space=pltpu.HBM)
    held = half // nrow
    piece = held // ncol if (held // ncol) % 16 == 0 else held
    grad_features, grad_weight = pl.pallas_call(
        functools.partial(hops, nrow, ncol, 1.0 / math.sqrt(side * places)),
        out_shape=(
            jax.ShapeDtypeStruct((side, half), BF16),
            jax.ShapeDtypeStruct((half, features), BF16),
        ),
        in_specs=[hbm] * 8,
        out_specs=(vmem, vmem),
        scratch_shapes=[
            pltpu.SMEM((1,), F32),
            pltpu.VMEM((side, half), BF16),
            pltpu.VMEM((half, features), BF16),
            pltpu.VMEM((side, half), BF16),
            pltpu.SMEM((1,), jnp.int32),
            pltpu.SMEM((slots,), jnp.int32),
            pltpu.SMEM((slots,), jnp.int32),
            pltpu.VMEM((slots, side, side), BF16),
            pltpu.SMEM((slots,), jnp.int32),
            pltpu.SMEM((slots,), jnp.int32),
            pltpu.SMEM((slots,), jnp.int32),
            pltpu.SMEM((slots,), jnp.int32),
            pltpu.SMEM((places,), jnp.int32),
            pltpu.VMEM((side, side), F32),
            pltpu.VMEM((slots + 1, side, side), BF16),
            pltpu.VMEM((half, side), BF16),
            pltpu.VMEM((2, CHUNKS, ncol, wide, side), BF16),
            pltpu.VMEM((CHUNKS, wide, side), F32),
            pltpu.VMEM((2, CHUNKS, nrow, wide, side), BF16),
            pltpu.VMEM((2, CHUNKS, nrow, wide, side), BF16),
            pltpu.VMEM((CHUNKS, 2, side, wide), BF16),
            pltpu.VMEM((CHUNKS, nrow, held, 2 * wide), BF16),
            pltpu.VMEM((CHUNKS, nrow, held, 2 * wide), BF16),
            pltpu.VMEM((CHUNKS, ncol, piece, 2 * wide), BF16),
            pltpu.VMEM((CHUNKS, held // piece, piece, 2 * wide), BF16),
            pltpu.VMEM((CHUNKS, nrow, held // piece, piece, 2 * wide), BF16),
            dma((8,)),
            dma((2, CHUNKS, ncol)), dma((2, CHUNKS, ncol)),
            dma((2, CHUNKS, nrow)), dma((2, CHUNKS, nrow)),
            dma((CHUNKS,)), dma((CHUNKS,)),
            dma((CHUNKS, nrow)), dma((CHUNKS, nrow)),
            dma((CHUNKS, ncol)), dma((CHUNKS, ncol)),
            dma((CHUNKS, nrow)), dma((CHUNKS, nrow)),
            dma((CHUNKS, ncol)), dma((CHUNKS, ncol)),
        ],
        compiler_params=pltpu.CompilerParams(
            collective_id=0, has_side_effects=True, vmem_limit_bytes=56 << 20),
    )(
        diffusion_time, node_features, weight, cotangent, tile_count.reshape(1),
        tile_row.reshape(slots), tile_col.reshape(slots), values)
    return pl.pallas_call(
        emit,
        out_shape=(
            jax.ShapeDtypeStruct((side, half), BF16),
            jax.ShapeDtypeStruct((half, features), F32),
        ),
        in_specs=[vmem, vmem],
        out_specs=(vmem, vmem),
        compiler_params=pltpu.CompilerParams(vmem_limit_bytes=60 << 20),
    )(grad_features, grad_weight)


def solution(mesh):
    return jax.shard_map(
        per_device,
        mesh=mesh,
        in_specs=(
            P(("row", "col"), "depth"),
            P("depth", None),
            P(("row", "col"), "depth"),
            P(),
            P("row", "col"),
            P("row", "col", None),
            P("row", "col", None),
            P("row", "col", None, None, None),
        ),
        out_specs=(P(("row", "col"), "depth"), P("depth", None)),
        check_vma=False,
    )
```

```python
import functools
import math

import jax
import jax.numpy as jnp
from jax import lax
from jax.experimental import pallas as pl
from jax.experimental.pallas import tpu as pltpu
from jax.sharding import PartitionSpec as P

MESH = pl.DeviceIdType.MESH
CHUNKS = 2
F32 = jnp.float32
BF16 = jnp.bfloat16


def hops(
    nrow, ncol, grad_scale,
    t_hbm, x_hbm, w_hbm, g_hbm, count_hbm, rows_hbm, cols_hbm, vals_hbm, gf_ref, gw_ref,
    t_ref, x_ref, w_ref, g_ref, count_ref, rows_ref, cols_ref, vals_ref,
    placed, rank, order, placed_at, tile_at, running, tiles,
    xt, source, total, part, got, h_all, gw_part, gw_got, gw_col, gw_back_to, gw_sum,
    load, g_s, g_r, p_s, p_r, d_s, d_r, w1_s, w1_r, w2_s, w2_r, w3_s, w3_r, w4_s, w4_r,
):
    row, col, depth = lax.axis_index("row"), lax.axis_index("col"), lax.axis_index("depth")
    side = g_ref.shape[0]
    slots = vals_ref.shape[0]
    wide = source.shape[3]
    places = nrow * ncol
    split = gw_col.shape[2] < gw_part.shape[2]

    loads = [
        pltpu.make_async_copy(src, dst, load.at[n])
        for n, (src, dst) in enumerate((
            (g_hbm, g_ref), (rows_hbm, rows_ref), (cols_hbm, cols_ref), (count_hbm, count_ref),
            (t_hbm, t_ref), (vals_hbm, vals_ref), (x_hbm, x_ref), (w_hbm, w_ref)))
    ]
    for copy in loads:
        copy.start()

    barrier = pltpu.get_barrier_semaphore()
    for i in range(1, nrow):
        pl.semaphore_signal(
            barrier, inc=1, device_id={"row": lax.rem(row + i, nrow)}, device_id_type=MESH)
    for i in range(1, ncol):
        pl.semaphore_signal(
            barrier, inc=1, device_id={"col": lax.rem(col + i, ncol)}, device_id_type=MESH)
    pl.semaphore_signal(barrier, inc=1, device_id={"depth": 1 - depth}, device_id_type=MESH)

    loads[0].wait()
    flipped = g_ref[...].astype(F32).T.astype(BF16)
    for k in range(CHUNKS):
        source[0, k, col] = flipped[k * wide:(k + 1) * wide, :]
    pl.semaphore_wait(barrier, nrow + ncol - 1)

    def to_col(ref, dst, send, recv, i):
        return pltpu.make_async_remote_copy(
            src_ref=ref, dst_ref=dst, send_sem=send, recv_sem=recv,
            device_id={"col": lax.rem(col + i, ncol)}, device_id_type=MESH)

    def to_row(ref, dst, send, recv, i):
        return pltpu.make_async_remote_copy(
            src_ref=ref, dst_ref=dst, send_sem=send, recv_sem=recv,
            device_id={"row": lax.rem(row + i, nrow)}, device_id_type=MESH)

    def spread(hop, k, i):
        piece = source.at[hop, k, col]
        return to_col(piece, piece, g_s.at[hop, k, i], g_r.at[hop, k, i], i)

    def partial(hop, k, i):
        return to_row(
            part.at[hop, k, lax.rem(row + i, nrow)], got.at[hop, k, row],
            p_s.at[hop, k, i], p_r.at[hop, k, i], i)

    def swap(k):
        piece = h_all.at[k, depth]
        return pltpu.make_async_remote_copy(
            src_ref=piece, dst_ref=piece, send_sem=d_s.at[k], recv_sem=d_r.at[k],
            device_id={"depth": 1 - depth}, device_id_type=MESH)

    def gw_rows(k, i):
        return to_row(
            gw_part.at[k, lax.rem(row + i, nrow)], gw_got.at[k, row],
            w1_s.at[k, i], w1_r.at[k, i], i)

    def gw_cols(k, i):
        mine = gw_back_to.at[k, lax.rem(col + i, ncol)] if split else gw_col.at[k, col]
        return to_col(mine, gw_col.at[k, col], w2_s.at[k, i], w2_r.at[k, i], i)

    def gw_share(k, i):
        piece = gw_sum.at[k, row, col]
        return to_col(piece, piece, w4_s.at[k, i], w4_r.at[k, i], i)

    def gw_back(k, i):
        piece = gw_sum.at[k, row]
        return to_row(piece, piece, w3_s.at[k, i], w3_r.at[k, i], i)

    def start_all(copy, n):
        for i in sorted(range(1, n), key=lambda i: -abs(2 * i - n)):
            copy(i).start()

    def recv_all(copy, n):
        for i in range(1, n):
            copy(i).wait_recv()

    def sent_all(copy, n):
        for i in range(1, n):
            copy(i).wait_send()

    def multiply(hop, k):
        recv_all(functools.partial(spread, hop, k), ncol)

        def target(i, carry):
            goal = lax.rem(row + i, nrow)
            terms = jnp.zeros((wide, side), F32)
            for p in range(ncol):
                terms += jnp.dot(
                    source[hop, k, p], tiles[tile_at[p * nrow + goal]],
                    preferred_element_type=F32)

            @pl.when(i < nrow)
            def _():
                part[hop, k, goal] = terms.astype(BF16)
                partial(hop, k, i).start()

            @pl.when(i == nrow)
            def _():
                total[k] = terms
            return carry

        lax.fori_loop(1, nrow + 1, target, 0)

    def collect(hop, k):
        recv_all(functools.partial(partial, hop, k), nrow)
        terms = total[k]
        for i in range(1, nrow):
            terms += got[hop, k, lax.rem(row + i, nrow)].astype(F32)
        return terms

    def spread_all(hop, k):
        if k > 0:
            sent_all(functools.partial(spread, hop, k - 1), ncol)
        start_all(functools.partial(spread, hop, k), ncol)

    spread_all(0, 0)

    for copy in loads[1:4]:
        copy.wait()
    live = count_ref[0]

    def enter(s, carry):
        placed[s] = jnp.where(s < live, rows_ref[s] * nrow + cols_ref[s], places)
        return carry

    lax.fori_loop(0, slots, enter, 0)

    def count_before(s, carry):
        mine = placed[s]
        before = jnp.int32(0)
        for other in range(slots):
            theirs = placed[other]
            ahead = (theirs < mine) | ((theirs == mine) & (other < s))
            before += jnp.where(ahead, 1, 0)
        rank[s] = before
        return carry

    lax.fori_loop(0, slots, count_before, 0)

    def invert(n, carry):
        slot, place = jnp.int32(0), jnp.int32(0)
        for s in range(slots):
            here = rank[s] == n
            slot += jnp.where(here, s, 0)
            place += jnp.where(here, placed[s], 0)
        order[n] = slot
        placed_at[n] = place
        return carry

    lax.fori_loop(0, slots, invert, 0)

    def find(p, carry):
        last, held = jnp.int32(-1), jnp.int32(0)
        for s in range(slots):
            last += jnp.where(placed[s] <= p, 1, 0)
            held += jnp.where(placed[s] == p, 1, 0)
        tile_at[p] = jnp.where(held > 0, last, slots)
        return carry

    lax.fori_loop(0, places, find, 0)
    loads[5].wait()
    running[...] = jnp.zeros_like(running)
    tiles[slots] = jnp.zeros((side, side), BF16)

    def add_up(n, carry):
        slot = order[n]
        same = placed_at[n] == placed_at[jnp.maximum(n - 1, 0)]
        keep = jnp.where(same, 1.0, 0.0).astype(F32)
        for b in range(0, side, 64):
            band = pl.ds(b, 64)
            now = running[band, :] * keep + vals_ref[slot, band, :].astype(F32)
            running[band, :] = now
            tiles[n, band, :] = now.astype(BF16)
        return carry

    lax.fori_loop(0, slots // 2, add_up, 0)
    for k in range(1, CHUNKS):
        spread_all(0, k)
    lax.fori_loop(slots // 2, slots, add_up, 0)
    for copy in loads[4:5] + loads[6:]:
        copy.wait()
    xt[...] = x_ref[...].astype(F32).T.astype(BF16)
    elapsed = t_ref[0]
    damping = jnp.exp(jnp.full((1, side), -elapsed, F32))
    coef_one = elapsed * damping
    coef_two = elapsed * elapsed * damping * 0.5

    def turn(k):
        source[1, k, col] = collect(0, k).astype(BF16)
        spread_all(1, k)

    def join(k):
        terms = (
            damping * source[0, k, col].astype(F32)
            + coef_one * source[1, k, col].astype(F32)
            + coef_two * collect(1, k))
        h_all[k, depth] = terms.T.astype(BF16)
        swap(k).start()

    def gw_begin(k):
        swap(k).wait_recv()
        for d in range(2):
            terms = jnp.dot(xt[...], h_all[k, d], preferred_element_type=F32) * grad_scale
            gw_part[k, :, :, d * wide:(d + 1) * wide] = terms.astype(BF16).reshape(
                nrow, side // nrow, wide)
        start_all(functools.partial(gw_rows, k), nrow)

    def gw_over_rows(k):
        recv_all(functools.partial(gw_rows, k), nrow)
        terms = gw_part[k, row].astype(F32)
        for i in range(1, nrow):
            terms += gw_got[k, lax.rem(row + i, nrow)].astype(F32)
        if split:
            gw_back_to[k] = terms.astype(BF16).reshape(gw_back_to.shape[1:])
            gw_col[k, col] = gw_back_to[k, col]
        else:
            gw_col[k, col] = terms.astype(BF16)
        start_all(functools.partial(gw_cols, k), ncol)

    def gw_over_cols(k):
        recv_all(functools.partial(gw_cols, k), ncol)
        terms = gw_col[k, 0].astype(F32)
        for j in range(1, ncol):
            terms += gw_col[k, j].astype(F32)
        if split:
            gw_sum[k, row, col] = terms.astype(BF16)
            start_all(functools.partial(gw_share, k), ncol)
        else:
            gw_sum[k, row, 0] = terms.astype(BF16)

    def gw_return(k):
        if split:
            recv_all(functools.partial(gw_share, k), ncol)
        start_all(functools.partial(gw_back, k), nrow)

    def gw_end(k):
        recv_all(functools.partial(gw_back, k), nrow)
        for d in range(2):
            at = (d * CHUNKS + k) * wide
            gw_ref[:, at:at + wide] = gw_sum[k, :, :, :, d * wide:(d + 1) * wide].reshape(
                side, wide)

    multiply(0, 0)
    turn(0)
    multiply(0, 1)
    turn(1)
    multiply(1, 0)
    join(0)
    multiply(1, 1)
    gw_begin(0)
    join(1)
    gw_over_rows(0)
    gw_begin(1)
    grad = jnp.zeros((side, side), F32)
    for k in range(CHUNKS):
        for d in range(2):
            at = (d * CHUNKS + k) * wide
            grad += lax.dot_general(
                h_all[k, d], w_ref[:, at:at + wide], (((1,), (1,)), ((), ())),
                preferred_element_type=F32)
    gf_ref[...] = grad.astype(BF16)
    gw_over_cols(0)
    gw_over_rows(1)
    gw_return(0)
    gw_over_cols(1)
    gw_return(1)
    for k in range(CHUNKS):
        gw_end(k)

    for k in range(CHUNKS):
        for hop in range(2):
            if k == CHUNKS - 1:
                sent_all(functools.partial(spread, hop, k), ncol)
            sent_all(functools.partial(partial, hop, k), nrow)
        swap(k).wait_send()
        for i in range(1, nrow):
            gw_rows(k, i).wait_send()
            gw_back(k, i).wait_send()
        for i in range(1, ncol):
            gw_cols(k, i).wait_send()
            if split:
                gw_share(k, i).wait_send()


def emit(gf_in, gw_in, gf_ref, gw_ref):
    gf_ref[...] = gf_in[...]
    gw_ref[...] = gw_in[...].astype(F32)


def per_device(
    node_features, weight, cotangent, diffusion_time, tile_count, tile_row, tile_col, tile_vals
):
    nrow, ncol = lax.axis_size("row"), lax.axis_size("col")
    values = tile_vals[0, 0]
    slots, side = values.shape[0], values.shape[-1]
    features = weight.shape[1]
    half = cotangent.shape[1]
    wide = half // CHUNKS
    places = nrow * ncol
    vmem = pl.BlockSpec(memory_space=pltpu.VMEM)

    dma = pltpu.SemaphoreType.DMA
    hbm = pl.BlockSpec(memory_space=pltpu.HBM)
    held = half // nrow
    piece = held
    grad_features, grad_weight = pl.pallas_call(
        functools.partial(hops, nrow, ncol, 1.0 / math.sqrt(side * places)),
        out_shape=(
            jax.ShapeDtypeStruct((side, half), BF16),
            jax.ShapeDtypeStruct((half, features), BF16),
        ),
        in_specs=[hbm] * 8,
        out_specs=(vmem, vmem),
        scratch_shapes=[
            pltpu.SMEM((1,), F32),
            pltpu.VMEM((side, half), BF16),
            pltpu.VMEM((half, features), BF16),
            pltpu.VMEM((side, half), BF16),
            pltpu.SMEM((1,), jnp.int32),
            pltpu.SMEM((slots,), jnp.int32),
            pltpu.SMEM((slots,), jnp.int32),
            pltpu.VMEM((slots, side, side), BF16),
            pltpu.SMEM((slots,), jnp.int32),
            pltpu.SMEM((slots,), jnp.int32),
            pltpu.SMEM((slots,), jnp.int32),
            pltpu.SMEM((slots,), jnp.int32),
            pltpu.SMEM((places,), jnp.int32),
            pltpu.VMEM((side, side), F32),
            pltpu.VMEM((slots + 1, side, side), BF16),
            pltpu.VMEM((half, side), BF16),
            pltpu.VMEM((2, CHUNKS, ncol, wide, side), BF16),
            pltpu.VMEM((CHUNKS, wide, side), F32),
            pltpu.VMEM((2, CHUNKS, nrow, wide, side), BF16),
            pltpu.VMEM((2, CHUNKS, nrow, wide, side), BF16),
            pltpu.VMEM((CHUNKS, 2, side, wide), BF16),
            pltpu.VMEM((CHUNKS, nrow, held, 2 * wide), BF16),
            pltpu.VMEM((CHUNKS, nrow, held, 2 * wide), BF16),
            pltpu.VMEM((CHUNKS, ncol, piece, 2 * wide), BF16),
            pltpu.VMEM((CHUNKS, held // piece, piece, 2 * wide), BF16),
            pltpu.VMEM((CHUNKS, nrow, held // piece, piece, 2 * wide), BF16),
            dma((8,)),
            dma((2, CHUNKS, ncol)), dma((2, CHUNKS, ncol)),
            dma((2, CHUNKS, nrow)), dma((2, CHUNKS, nrow)),
            dma((CHUNKS,)), dma((CHUNKS,)),
            dma((CHUNKS, nrow)), dma((CHUNKS, nrow)),
            dma((CHUNKS, ncol)), dma((CHUNKS, ncol)),
            dma((CHUNKS, nrow)), dma((CHUNKS, nrow)),
            dma((CHUNKS, ncol)), dma((CHUNKS, ncol)),
        ],
        compiler_params=pltpu.CompilerParams(
            collective_id=0, has_side_effects=True, vmem_limit_bytes=56 << 20),
    )(
        diffusion_time, node_features, weight, cotangent, tile_count.reshape(1),
        tile_row.reshape(slots), tile_col.reshape(slots), values)
    return pl.pallas_call(
        emit,
        out_shape=(
            jax.ShapeDtypeStruct((side, half), BF16),
            jax.ShapeDtypeStruct((half, features), F32),
        ),
        in_specs=[vmem, vmem],
        out_specs=(vmem, vmem),
        compiler_params=pltpu.CompilerParams(vmem_limit_bytes=60 << 20),
    )(grad_features, grad_weight)


def solution(mesh):
    return jax.shard_map(
        per_device,
        mesh=mesh,
        in_specs=(
            P(("row", "col"), "depth"),
            P("depth", None),
            P(("row", "col"), "depth"),
            P(),
            P("row", "col"),
            P("row", "col", None),
            P("row", "col", None),
            P("row", "col", None, None, None),
        ),
        out_specs=(P(("row", "col"), "depth"), P("depth", None)),
        check_vma=False,
    )
```
